32 devices in a mesh: groups: 2 (over y), expert: 8 (over z, x), head: 2 (over core).
Axes of the slice: x: 2, y: 2, z: 4, core: 2. Of those that a mesh axis runs over, the one named last changes fastest.
Arguments:
- moe_in: bfloat16 [128, 7168], P(('groups', 'expert'), 'head'), parts along dimension 0, may hold values from -6 to 6
- routes: int32 [128, 2], P(('groups', 'expert')), parts along dimension 0, may hold values from 0 to 7, all different within a row; in each aligned block of 8 rows (0 to 7, 8 to 15, ...) at most 2 rows name the same one
- gate_weights: float32 [128, 2], P(('groups', 'expert')), parts along dimension 0, may hold values from 0.1 to 1
- w_gate: bfloat16 [7168, 16384], P('head', 'expert'), may hold values from -0.0625 to 0.0625
- w_up: bfloat16 [7168, 16384], P('head', 'expert'), may hold values from -0.0625 to 0.0625
- w_down: bfloat16 [16384, 7168], P('expert', 'head'), may hold values from -0.125 to 0.125
Outputs:
- moe_out: bfloat16 [128, 7168], P(('groups', 'expert'), 'head'), parts along dimension 0
The draws below stay inside these ranges and needn't reach their ends.
There are 2 independent parts, one for each index of `groups`. The reference program is written for one: setup_inputs(seed, part) draws one part's arguments, and reference() takes and returns one part's arrays. A program takes and returns all parts, laid end to end along the dimension named above; an argument that names none is the same for every part. Nothing has to cross between parts.
Inputs may be any that keep to these rules, and one draw needn't show every extreme that they name: `routes`: each row names 2 different experts; among the 8 rows of one device no expert is named more than 2 times, a bound that some block reaches.
All inputs are finite; a program needn't handle non-finite values.
Results may differ from the reference program's by a relative error of at most 0.0058.
Values may be sent and summed in bfloat16 or wider, within the bound.
No kernel may reach another device: no remote copies, remote signals or barrier semaphores. Data moves between devices by JAX's collectives and lax.ppermute only.
A program may use at most 128 MiB of HBM per device.

```python
import math
import jax
import jax.numpy as jnp
import numpy as np
from jax import lax

D = 7168
FF = 2048
FLIGHT = 8
TOPK = 2
RM = 8
CAP = 2
MOE_ROWS = 64
COLS = 16384
N_EXPERT = 8


def block_scale(key, extent, pieces, low, high):
    gain = 1.0
    for dim, parts in pieces:
        heights = jax.random.uniform(jax.random.fold_in(jax.random.fold_in(key, 6), dim), (parts,), jnp.float32, low / len(pieces), high / len(pieces))
        gain = gain * jnp.repeat(jnp.exp(heights), extent[dim] // parts).reshape((-1,) + (1,) * (len(extent) - 1 - dim))
    return gain


def shared_out(own_key, own, number, rows, amount, top, reach, lean):
    ranking = jax.random.permutation(own_key, amount)
    crowded, common = load_shares(amount, rows * top, reach, lean, True), load_shares(amount, rows * top, reach, lean, False)
    places = jnp.arange(amount)

    def named(lengths, turn):
        used = int((lengths > 0).sum())
        fixed = max(1, used // 4)
        moved = fixed + (places - fixed + turn * (used - fixed)) % max(1, amount - fixed)
        return jnp.zeros((amount,), jnp.int32).at[ranking[jnp.where(places < fixed, places, moved)]].set(jnp.asarray(lengths, jnp.int32))

    lengths = jnp.where(number % 4 == 0, named(crowded, number // 4), named(common, number - number // 4 - 1))
    mixed = jax.random.permutation(jax.random.fold_in(own, 3), amount)
    donor, sink = mixed[0:amount // 2 * 2:2], mixed[1:amount // 2 * 2:2]
    margin = jnp.minimum(lengths[donor] - 1, reach - lengths[sink]) // 2
    margin = jnp.where((donor == ranking[0]) | (sink == ranking[0]) | (lengths[sink] == 0), 0, jnp.maximum(margin, 0))
    moved = jax.random.randint(jax.random.fold_in(own, 4), (amount // 2,), 0, 1 << 20) % (margin + 1)
    lengths = lengths.at[donor].add(-moved).at[sink].add(moved)
    labels = jnp.searchsorted(jnp.cumsum(lengths), jnp.arange(rows * top), side="right").astype(jnp.int32)
    grid = labels.reshape(top, rows).T
    grid = grid[jax.random.permutation(jax.random.fold_in(own, 1), rows)]
    turn = jax.random.randint(jax.random.fold_in(own, 2), (rows, 1), 0, top)
    return jnp.take_along_axis(grid, (jnp.arange(top)[None, :] + turn) % top, axis=1)


def load_shares(number_of, total, limit, lean, full):
    portions = [(1 << 20) // math.isqrt(standing ** lean) + 1 for standing in range(1, number_of + 1)]
    largest = limit if full else min(limit, max(-(-total // number_of), total * portions[0] // sum(portions)))
    least = 1 if total - largest >= number_of - 1 else 0
    counts, rest = [largest] + [least] * (number_of - 1), total - largest - least * (number_of - 1)
    while rest > 0:
        candidates = [i for i in range(1, number_of) if counts[i] < largest] or [i for i in range(1, number_of) if counts[i] < limit]
        pool, remaining = sum([portions[i] for i in candidates]), rest
        for i in candidates:
            addition = min(limit - counts[i], max(1, remaining * portions[i] // pool), rest)
            counts[i] = counts[i] + addition
            rest = rest - addition
    return np.array(counts)


def noise(stream_key, extent, spread, bound, split=(), kind=jnp.bfloat16):
    array = spread * jax.random.normal(stream_key, extent, jnp.float32)
    if split:
        array = array * block_scale(stream_key, extent, split, -0.22, 0.18)
    return jnp.clip(array, -bound, bound).astype(kind)


def setup_inputs(seed: int = 0, part: int = 0) -> dict:
    seeds = jax.random.split(jax.random.key(seed), 7)
    part_keys = jax.random.split(jax.random.fold_in(seeds[6], part), 7)
    moe_in = noise(part_keys[0], (MOE_ROWS, D), 1.0, 6.0, ((0, 8), (1, 2)))
    routes_keys = jax.random.split(jax.random.fold_in(part_keys[1], 1), MOE_ROWS // RM)
    routes_turns = jax.random.permutation(jax.random.fold_in(part_keys[1], 3), MOE_ROWS // RM)
    routes = jax.vmap(lambda own, number: shared_out(jax.random.fold_in(part_keys[1], 2), own, number, RM, FLIGHT, TOPK, CAP, 2))(routes_keys, routes_turns).reshape((MOE_ROWS, TOPK))
    gate_weights = jnp.clip(0.1 + 0.9 * jax.random.uniform(part_keys[2], (MOE_ROWS, TOPK), jnp.float32) ** block_scale(part_keys[2], (MOE_ROWS, TOPK), ((0, 8),), -0.2, 0.2), 0.1, 1.0)
    w_gate = noise(seeds[3], (D, COLS), D ** -0.5, 0.0625, ((0, 2), (1, 8)))
    w_up = noise(seeds[4], (D, COLS), D ** -0.5, 0.0625, ((0, 2), (1, 8)))
    w_down = noise(seeds[5], (COLS, D), FF ** -0.5, 0.125, ((0, 8), (1, 2)))
    return {"moe_in": moe_in, "routes": routes, "gate_weights": gate_weights, "w_gate": w_gate, "w_up": w_up, "w_down": w_down}


def experts(moe_in, routes, gate_weights, w_gate, w_up, w_down):
    split_count = N_EXPERT // FLIGHT
    slice_width = FF // split_count
    row_bound = N_EXPERT * CAP

    def one_expert(carry, expert):
        matched = routes == expert
        chosen = jnp.any(matched, axis=1)
        gate_hit = jnp.sum(jnp.where(matched, gate_weights, 0.0), axis=1)
        sorting = jnp.argsort(jnp.where(chosen, 0, 1).astype(jnp.int32), stable=True)[:row_bound].astype(jnp.int32)
        picked = moe_in[sorting]
        gate_cols = lax.dynamic_slice_in_dim(w_gate, expert * FF, FF, 1)
        up_cols = lax.dynamic_slice_in_dim(w_up, expert * FF, FF, 1)
        gate_pre = jnp.dot(picked, gate_cols, preferred_element_type=jnp.float32)
        up_pre = jnp.dot(picked, up_cols, preferred_element_type=jnp.float32)
        hidden = (jax.nn.silu(gate_pre) * up_pre).astype(jnp.bfloat16)
        down_rows = lax.dynamic_slice_in_dim(w_down, expert * FF, FF, 0)
        slice_out = jnp.einsum(
            "rsh,shd->rsd",
            hidden.reshape(row_bound, split_count, slice_width).astype(jnp.float32),
            down_rows.reshape(split_count, slice_width, D).astype(jnp.float32),
        )
        rounded = lax.optimization_barrier(slice_out.astype(jnp.bfloat16))
        expert_out = jnp.sum(rounded.astype(jnp.float32), axis=1)
        contrib = expert_out * gate_hit[sorting][:, None]
        return carry.at[sorting].add(contrib), None

    start = jnp.zeros(moe_in.shape, jnp.float32)
    summed, unused = lax.scan(one_expert, start, jnp.arange(FLIGHT, dtype=jnp.int32))
    return summed.astype(jnp.bfloat16)


def reference(moe_in, routes, gate_weights, w_gate, w_up, w_down):
    return experts(moe_in, routes, gate_weights, w_gate, w_up, w_down)
```

```python
import jax
import jax.numpy as jnp
from jax import lax
from jax.sharding import PartitionSpec as P

FLIGHT = 8
CAP = 2


def per_device(moe_in, routes, gate_weights, w_gate, w_up, w_down):
    expert_ids = jnp.arange(FLIGHT, dtype=jnp.int32)
    matched = (routes[:, :, None] == expert_ids[None, None, :]).astype(jnp.float32)
    chosen = jnp.sum(matched, axis=1)
    gate_hit = jnp.sum(matched * gate_weights[:, :, None], axis=1)
    slot_index = jnp.cumsum(chosen, axis=0) - chosen
    slot_ids = jnp.arange(CAP, dtype=jnp.float32)
    placing = chosen[:, :, None] * (slot_index[:, :, None] == slot_ids[None, None, :]).astype(
        jnp.float32
    )
    packed_rows = jnp.einsum(
        "rfc,rd->fcd", placing.astype(jnp.bfloat16), moe_in, preferred_element_type=jnp.float32
    ).astype(jnp.bfloat16)
    copies = lax.axis_size("expert") // FLIGHT
    width = moe_in.shape[1]
    outgoing = jnp.broadcast_to(packed_rows[:, None], (FLIGHT, copies, CAP, width)).reshape(
        FLIGHT * copies, CAP, width
    )
    arrived = lax.all_to_all(outgoing, "expert", split_axis=0, concat_axis=0, tiled=True)
    sources, count, features = arrived.shape
    arrived_rows = arrived.reshape(sources * count, features)
    gate_part = jnp.dot(arrived_rows, w_gate, preferred_element_type=jnp.float32)
    up_part = jnp.dot(arrived_rows, w_up, preferred_element_type=jnp.float32)
    cores = lax.axis_size("head")
    swap = [(i, (i + 1) % cores) for i in range(cores)]
    gate_pre = gate_part + lax.ppermute(gate_part, "head", swap)
    up_pre = up_part + lax.ppermute(up_part, "head", swap)
    hidden = (jax.nn.silu(gate_pre) * up_pre).astype(jnp.bfloat16)
    partial_out = jnp.dot(hidden, w_down, preferred_element_type=jnp.float32).astype(jnp.bfloat16)
    returned = lax.all_to_all(
        partial_out.reshape(sources, count, features),
        "expert",
        split_axis=0,
        concat_axis=0,
        tiled=True,
    )
    summed = jnp.sum(returned.reshape(FLIGHT, copies, CAP, width).astype(jnp.float32), axis=1)
    spread = placing * gate_hit[:, :, None]
    moe_out = jnp.einsum("rfc,fcd->rd", spread, summed, precision=lax.Precision.HIGHEST).astype(
        jnp.bfloat16
    )
    return moe_out


def solution(mesh):
    in_specs = (
        P(("groups", "expert"), "head"),
        P(("groups", "expert"), None),
        P(("groups", "expert"), None),
        P("head", "expert"),
        P("head", "expert"),
        P("expert", "head"),
    )
    out_specs = P(("groups", "expert"), "head")
    return jax.shard_map(
        per_device, mesh=mesh, in_specs=in_specs, out_specs=out_specs, check_vma=False
    )
```

```python
import functools

import jax
import jax.numpy as jnp
from jax import lax
from jax.experimental import pallas as pl
from jax.experimental.pallas import tpu as pltpu
from jax.sharding import PartitionSpec as P

FLIGHT = 8
CAP = 2
TILE = 512
AHEAD = 450
SMALL = pltpu.CompilerParams(vmem_limit_bytes=4 << 20)
VMEM = pl.BlockSpec(memory_space=pltpu.VMEM)


def near(array):
    return pltpu.with_memory_space_constraint(array, pltpu.VMEM)


def call(kernel, out_shape, *operands, flops=0):
    return pl.pallas_call(
        kernel,
        out_shape=out_shape,
        in_specs=[VMEM] * len(operands),
        out_specs=jax.tree.map(lambda _: VMEM, out_shape),
        compiler_params=SMALL,
        cost_estimate=pl.CostEstimate(flops=flops, bytes_accessed=0, transcendentals=0),
        name=kernel.__name__,
    )(*operands)


def placing(routes, slots):
    rows = routes.shape[1]
    slot = lax.broadcasted_iota(jnp.int32, (slots, rows), 0)
    expert = lax.div(slot, CAP)
    chosen = (routes[0:1, :] == expert).astype(jnp.float32)
    for k in range(1, routes.shape[0]):
        chosen += (routes[k : k + 1, :] == expert).astype(jnp.float32)
    earlier = (
        lax.broadcasted_iota(jnp.int32, (rows, rows), 0)
        < lax.broadcasted_iota(jnp.int32, (rows, rows), 1)
    ).astype(jnp.float32)
    rank = jnp.dot(chosen, earlier, preferred_element_type=jnp.float32)
    return chosen * (rank == (slot - expert * CAP).astype(jnp.float32)).astype(jnp.float32)


def pack(routes_ref, rows_ref, out_ref):
    experts, cap, width = out_ref.shape
    place = placing(routes_ref[...], experts * cap).astype(jnp.bfloat16)
    packed = jnp.dot(place, rows_ref[...], preferred_element_type=jnp.float32).astype(
        out_ref.dtype
    )
    out_ref[...] = packed.reshape(out_ref.shape)


def gate_up(rows_ref, gate_ref, up_ref, gate_out, up_out):
    columns = gate_ref.shape[1]
    tile = min(TILE, columns)
    rows = rows_ref[...].reshape(-1, rows_ref.shape[-1])

    @pl.loop(0, columns // tile)
    def _(i):
        at = pl.ds(pl.multiple_of(i * tile, tile), tile)
        gate_out[:, at] = jnp.dot(rows, gate_ref[:, at], preferred_element_type=jnp.float32)
        up_out[:, at] = jnp.dot(rows, up_ref[:, at], preferred_element_type=jnp.float32)


def down(gate_ref, gate_other, up_ref, up_other, down_ref, out_ref):
    gate = gate_ref[...] + gate_other[...]
    up = up_ref[...] + up_other[...]
    hidden = (gate / (1.0 + jnp.exp(-gate)) * up).astype(jnp.bfloat16)
    columns = down_ref.shape[1]
    tile = min(TILE, columns)

    @pl.loop(0, columns // tile)
    def _(i):
        at = pl.ds(pl.multiple_of(i * tile, tile), tile)
        part = jnp.dot(hidden, down_ref[:, at], preferred_element_type=jnp.float32)
        out_ref[:, :, at] = part.astype(out_ref.dtype).reshape(*out_ref.shape[:2], tile)


def unpack(routes_ref, gates_ref, slots_ref, out_ref):
    experts, cap, width = slots_ref.shape
    routes = routes_ref[...]
    gates = gates_ref[...]
    place = placing(routes, experts * cap)
    slot = lax.broadcasted_iota(jnp.int32, place.shape, 0)
    expert = lax.div(slot, CAP)
    weight = jnp.zeros(place.shape, jnp.float32)
    for k in range(routes.shape[0]):
        weight += jnp.where(routes[k : k + 1, :] == expert, gates[k : k + 1, :], 0.0)
    out_ref[...] = lax.dot_general(
        place * weight,
        slots_ref[...].reshape(experts * cap, width).astype(jnp.float32),
        (((0,), (0,)), ((), ())),
        precision=lax.Precision.HIGHEST,
        preferred_element_type=jnp.float32,
    ).astype(out_ref.dtype)


def per_device(moe_in, routes, gate_weights, w_gate, w_up, w_down):
    rows, width = moe_in.shape
    routes_t, gates_t = routes.T, gate_weights.T
    n = lax.axis_size("expert")
    copies = n // FLIGHT
    outgoing = call(
        pack, jax.ShapeDtypeStruct((FLIGHT, CAP, width), moe_in.dtype), routes_t, moe_in,
        flops=AHEAD * (w_gate.nbytes + w_up.nbytes + w_down.nbytes),
    )
    if copies > 1:
        outgoing = jnp.broadcast_to(outgoing[:, None], (FLIGHT, copies, CAP, width)).reshape(
            n, CAP, width
        )
    arrived = lax.all_to_all(outgoing, "expert", split_axis=0, concat_axis=0, tiled=True)
    pre = jax.ShapeDtypeStruct((n * CAP, w_gate.shape[1]), jnp.float32)
    gate_part, up_part = call(
        gate_up, (pre, pre), arrived, near(w_gate), near(w_up), flops=4 * n * CAP * w_gate.size
    )
    cores = lax.axis_size("head")
    swap = [(i, (i + 1) % cores) for i in range(cores)]
    gate_other, up_other = (lax.ppermute(x, "head", swap) for x in (gate_part, up_part))
    partial_out = call(
        down,
        jax.ShapeDtypeStruct((n, CAP, width), moe_in.dtype),
        gate_part, gate_other, up_part, up_other, near(w_down),
        flops=2 * n * CAP * w_down.size,
    )
    returned = lax.all_to_all(partial_out, "expert", split_axis=0, concat_axis=0, tiled=True)
    if copies > 1:
        returned = jnp.sum(
            returned.reshape(FLIGHT, copies, CAP, width).astype(jnp.float32), axis=1
        )
    return call(unpack, jax.ShapeDtypeStruct((rows, width), moe_in.dtype), routes_t, gates_t, returned)


def solution(mesh):
    in_specs = (
        P(("groups", "expert"), "head"),
        P(("groups", "expert"), None),
        P(("groups", "expert"), None),
        P("head", "expert"),
        P("head", "expert"),
        P("expert", "head"),
    )
    out_specs = P(("groups", "expert"), "head")
    return jax.shard_map(
        per_device, mesh=mesh, in_specs=in_specs, out_specs=out_specs, check_vma=False
    )
```

```python
import functools

import jax
import jax.numpy as jnp
from jax import lax
from jax.experimental import pallas as pl
from jax.experimental.pallas import tpu as pltpu
from jax.sharding import PartitionSpec as P

FLIGHT = 8
CAP = 2
TILE = 512
LANES = 128
AHEAD = 300
SMALL = pltpu.CompilerParams(vmem_limit_bytes=4 << 20)
VMEM = pl.BlockSpec(memory_space=pltpu.VMEM)


def near(array):
    return pltpu.with_memory_space_constraint(array, pltpu.VMEM)


def far(array):
    return pltpu.with_memory_space_constraint(array, pltpu.HBM)


def call(kernel, out_shape, *operands, flops=0):
    return pl.pallas_call(
        kernel,
        out_shape=out_shape,
        in_specs=[VMEM] * len(operands),
        out_specs=jax.tree.map(lambda _: VMEM, out_shape),
        compiler_params=SMALL,
        cost_estimate=pl.CostEstimate(flops=flops, bytes_accessed=0, transcendentals=0),
        name=getattr(kernel, "func", kernel).__name__,
    )(*operands)


def placing(routes, slots):
    rows = routes.shape[1]
    slot = lax.broadcasted_iota(jnp.int32, (slots, rows), 0)
    expert = lax.div(slot, CAP)
    chosen = (routes[0:1, :] == expert).astype(jnp.float32)
    for k in range(1, routes.shape[0]):
        chosen += (routes[k : k + 1, :] == expert).astype(jnp.float32)
    earlier = (
        lax.broadcasted_iota(jnp.int32, (rows, rows), 0)
        < lax.broadcasted_iota(jnp.int32, (rows, rows), 1)
    ).astype(jnp.float32)
    rank = jnp.dot(chosen, earlier, preferred_element_type=jnp.float32)
    return chosen * (rank == (slot - expert * CAP).astype(jnp.float32)).astype(jnp.float32)


def pack(routes_hbm, rows_hbm, out_ref, routes_ref, rows_ref, sems):
    loads = [
        pltpu.make_async_copy(routes_hbm, routes_ref, sems.at[0]),
        pltpu.make_async_copy(rows_hbm, rows_ref, sems.at[1]),
    ]
    for load in loads:
        load.start()
    loads[0].wait()
    experts, cap, width = out_ref.shape
    place = placing(routes_ref[...], experts * cap).astype(jnp.bfloat16)
    loads[1].wait()
    packed = jnp.dot(place, rows_ref[...], preferred_element_type=jnp.float32).astype(
        out_ref.dtype
    )
    out_ref[...] = packed.reshape(out_ref.shape)


def gate_up(part, rows_ref, gate_ref, up_ref, out_ref):
    columns = out_ref.shape[2]
    tile = min(TILE, columns)
    rows = rows_ref[...].reshape(-1, rows_ref.shape[-1])
    for start in range(0, columns, tile):
        for k, weights in enumerate((gate_ref, up_ref)):
            out_ref[k, :, start : start + tile] = jnp.dot(
                rows,
                weights[:, part * columns + start : part * columns + start + tile],
                preferred_element_type=jnp.float32,
            )


def spread(routes, gates, slots):
    place = placing(routes, slots)
    expert = lax.div(lax.broadcasted_iota(jnp.int32, place.shape, 0), CAP)
    weight = jnp.zeros(place.shape, jnp.float32)
    for k in range(routes.shape[0]):
        weight += jnp.where(routes[k : k + 1, :] == expert, gates[k : k + 1, :], 0.0)
    rest, terms = place * weight, []
    for _ in range(3):
        terms.append(rest.astype(jnp.bfloat16))
        rest = rest - terms[-1].astype(jnp.float32)
    return jnp.concatenate(terms, axis=1)


def down(part, last, down_ref, own_ref, other_ref, *refs):
    columns = own_ref.shape[2]
    gate = own_ref[0] + other_ref[0]
    up = own_ref[1] + other_ref[1]
    hidden = (gate / (1.0 + jnp.exp(-gate)) * up).astype(jnp.bfloat16)
    width = down_ref.shape[1]
    tile = min(TILE, width)
    if last:
        *totals, routes_ref, gates_ref, out_ref, terms_ref = refs
        terms_ref[...] = spread(routes_ref[...], gates_ref[...], terms_ref.shape[0])
    else:
        *totals, out_ref = refs
    for start in range(0, width, tile):
        at = slice(start, start + tile)
        total = jnp.dot(
            hidden,
            down_ref[part * columns : (part + 1) * columns, at],
            preferred_element_type=jnp.float32,
        )
        if totals:
            total += totals[0][:, at]
        out_ref[..., at] = total.astype(out_ref.dtype).reshape(*out_ref.shape[:-1], tile)


def unpack(terms_ref, slots_ref, out_ref):
    experts, cap, width = slots_ref.shape
    sums = lax.dot_general(
        terms_ref[...],
        slots_ref[...].astype(jnp.bfloat16).reshape(experts * cap, width),
        (((0,), (0,)), ((), ())),
        preferred_element_type=jnp.float32,
    )
    rows = out_ref.shape[0]
    out_ref[...] = (sums[:rows] + sums[rows : 2 * rows] + sums[2 * rows :]).astype(out_ref.dtype)


def per_device(moe_in, routes, gate_weights, w_gate, w_up, w_down):
    rows, width = moe_in.shape
    routes_t, gates_t = routes.T, gate_weights.T
    n = lax.axis_size("expert")
    copies = n // FLIGHT
    outgoing = pl.pallas_call(
        pack,
        out_shape=jax.ShapeDtypeStruct((FLIGHT, CAP, width), moe_in.dtype),
        in_specs=[pl.BlockSpec(memory_space=pltpu.HBM)] * 2,
        out_specs=VMEM,
        scratch_shapes=[
            pltpu.VMEM(routes_t.shape, routes_t.dtype),
            pltpu.VMEM(moe_in.shape, moe_in.dtype),
            pltpu.SemaphoreType.DMA((2,)),
        ],
        compiler_params=SMALL,
        cost_estimate=pl.CostEstimate(
            flops=AHEAD * (w_gate.nbytes + w_up.nbytes + w_down.nbytes),
            bytes_accessed=0,
            transcendentals=0,
        ),
        name="pack",
    )(far(routes_t), far(moe_in))
    if copies > 1:
        outgoing = jnp.broadcast_to(outgoing[:, None], (FLIGHT, copies, CAP, width)).reshape(
            n, CAP, width
        )
    arrived = lax.all_to_all(outgoing, "expert", split_axis=0, concat_axis=0, tiled=True)
    columns = w_gate.shape[1]
    parts = 2 if columns % (2 * LANES) == 0 else 1
    cores = lax.axis_size("head")
    swap = [(i, (i + 1) % cores) for i in range(cores)]
    near_gate, near_up, near_down = near(w_gate), near(w_up), near(w_down)
    own, other = [], []
    for part in range(parts):
        own.append(
            call(
                functools.partial(gate_up, part),
                jax.ShapeDtypeStruct((2, n * CAP, columns // parts), jnp.float32),
                arrived, near_gate, near_up,
                flops=4 * n * CAP * w_gate.size // parts,
            )
        )
        other.append(lax.ppermute(own[-1], "head", swap))
    totals = ()
    for part in range(parts - 1):
        totals = (
            call(
                functools.partial(down, part, False),
                jax.ShapeDtypeStruct((n * CAP, width), jnp.float32),
                near_down, own[part], other[part], *totals,
                flops=2 * n * CAP * w_down.size // parts,
            ),
        )
    partial_out, terms = call(
        functools.partial(down, parts - 1, True),
        (
            jax.ShapeDtypeStruct((n, CAP, width), moe_in.dtype),
            jax.ShapeDtypeStruct((FLIGHT * CAP, 3 * rows), jnp.bfloat16),
        ),
        near_down, own[-1], other[-1], *totals, routes_t, gates_t,
        flops=2 * n * CAP * w_down.size // parts,
    )
    returned = lax.all_to_all(partial_out, "expert", split_axis=0, concat_axis=0, tiled=True)
    if copies > 1:
        returned = jnp.sum(
            returned.reshape(FLIGHT, copies, CAP, width).astype(jnp.float32), axis=1
        )
    return call(unpack, jax.ShapeDtypeStruct((rows, width), moe_in.dtype), terms, returned)


def solution(mesh):
    in_specs = (
        P(("groups", "expert"), "head"),
        P(("groups", "expert"), None),
        P(("groups", "expert"), None),
        P("head", "expert"),
        P("head", "expert"),
        P("expert", "head"),
    )
    out_specs = P(("groups", "expert"), "head")
    return jax.shard_map(
        per_device, mesh=mesh, in_specs=in_specs, out_specs=out_specs, check_vma=False
    )
```

```python
import functools

import jax
import jax.numpy as jnp
from jax import lax
from jax.experimental import pallas as pl
from jax.experimental.pallas import tpu as pltpu
from jax.sharding import PartitionSpec as P

FLIGHT = 8
CAP = 2
TILE = 512
LANES = 128
ORDERS = {8: (4, 2, 7, 6, 0, 1, 3, 5)}
AHEAD = 300
SMALL = pltpu.CompilerParams(vmem_limit_bytes=4 << 20)
VMEM = pl.BlockSpec(memory_space=pltpu.VMEM)


def near(array):
    return pltpu.with_memory_space_constraint(array, pltpu.VMEM)


def far(array):
    return pltpu.with_memory_space_constraint(array, pltpu.HBM)


def call(kernel, out_shape, *operands, flops=0):
    return pl.pallas_call(
        kernel,
        out_shape=out_shape,
        in_specs=[VMEM] * len(operands),
        out_specs=jax.tree.map(lambda _: VMEM, out_shape),
        compiler_params=SMALL,
        cost_estimate=pl.CostEstimate(flops=flops, bytes_accessed=0, transcendentals=0),
        name=getattr(kernel, "func", kernel).__name__,
    )(*operands)


def experts_of(order, shape):
    slot = lax.broadcasted_iota(jnp.int32, shape, 0)
    block = lax.div(slot, CAP)
    expert = jnp.zeros(shape, jnp.int32)
    for place, name in enumerate(order):
        expert = jnp.where(block == place, name, expert)
    return expert, slot - block * CAP


def placing(routes, order):
    rows = routes.shape[1]
    expert, number = experts_of(order, (len(order) * CAP, rows))
    chosen = (routes[0:1, :] == expert).astype(jnp.float32)
    for k in range(1, routes.shape[0]):
        chosen += (routes[k : k + 1, :] == expert).astype(jnp.float32)
    earlier = (
        lax.broadcasted_iota(jnp.int32, (rows, rows), 0)
        < lax.broadcasted_iota(jnp.int32, (rows, rows), 1)
    ).astype(jnp.float32)
    rank = jnp.dot(chosen, earlier, preferred_element_type=jnp.float32)
    return chosen * (rank == number.astype(jnp.float32)).astype(jnp.float32)


def pack(order, routes_hbm, rows_hbm, out_ref, routes_ref, rows_ref, sems):
    loads = [
        pltpu.make_async_copy(routes_hbm, routes_ref, sems.at[0]),
        pltpu.make_async_copy(rows_hbm, rows_ref, sems.at[1]),
    ]
    for load in loads:
        load.start()
    loads[0].wait()
    place = placing(routes_ref[...], order).astype(jnp.bfloat16)
    loads[1].wait()
    packed = jnp.dot(place, rows_ref[...], preferred_element_type=jnp.float32).astype(
        out_ref.dtype
    )
    out_ref[...] = packed.reshape(out_ref.shape)


def gate_up(part, rows_ref, gate_ref, up_ref, out_ref):
    columns = out_ref.shape[2]
    tile = min(TILE, columns)
    rows = rows_ref[...].reshape(-1, rows_ref.shape[-1])
    for start in range(0, columns, tile):
        for k, weights in enumerate((gate_ref, up_ref)):
            out_ref[k, :, start : start + tile] = jnp.dot(
                rows,
                weights[:, part * columns + start : part * columns + start + tile],
                preferred_element_type=jnp.float32,
            )


def spread(routes, gates, order):
    place = placing(routes, order)
    expert, _ = experts_of(order, place.shape)
    weight = jnp.zeros(place.shape, jnp.float32)
    for k in range(routes.shape[0]):
        weight += jnp.where(routes[k : k + 1, :] == expert, gates[k : k + 1, :], 0.0)
    rest, terms = place * weight, []
    for _ in range(3):
        terms.append(rest.astype(jnp.bfloat16))
        rest = rest - terms[-1].astype(jnp.float32)
    return jnp.concatenate(terms, axis=1)


def down(part, order, down_ref, own_ref, other_ref, *refs):
    columns = own_ref.shape[2]
    gate = own_ref[0] + other_ref[0]
    up = own_ref[1] + other_ref[1]
    hidden = (gate / (1.0 + jnp.exp(-gate)) * up).astype(jnp.bfloat16)
    width = down_ref.shape[1]
    tile = min(TILE, width)
    if order:
        *totals, routes_ref, gates_ref, out_ref, terms_ref = refs
        terms_ref[...] = spread(routes_ref[...], gates_ref[...], order)
    else:
        *totals, out_ref = refs
    for start in range(0, width, tile):
        at = slice(start, start + tile)
        total = jnp.dot(
            hidden,
            down_ref[part * columns : (part + 1) * columns, at],
            preferred_element_type=jnp.float32,
        )
        if totals:
            total += totals[0][:, at]
        out_ref[..., at] = total.astype(out_ref.dtype).reshape(*out_ref.shape[:-1], tile)


def unpack(terms_ref, slots_ref, out_ref):
    experts, cap, width = slots_ref.shape
    sums = lax.dot_general(
        terms_ref[...],
        slots_ref[...].astype(jnp.bfloat16).reshape(experts * cap, width),
        (((0,), (0,)), ((), ())),
        preferred_element_type=jnp.float32,
    )
    rows = out_ref.shape[0]
    out_ref[...] = (sums[:rows] + sums[rows : 2 * rows] + sums[2 * rows :]).astype(out_ref.dtype)


def per_device(moe_in, routes, gate_weights, w_gate, w_up, w_down):
    rows, width = moe_in.shape
    routes_t, gates_t = routes.T, gate_weights.T
    n = lax.axis_size("expert")
    copies = n // FLIGHT
    order = ORDERS.get(n, tuple(range(FLIGHT)))
    exchange = functools.partial(
        lax.all_to_all, axis_name="expert", split_axis=0, concat_axis=0, tiled=True,
        axis_index_groups=[list(order)] if copies == 1 else None,
    )
    outgoing = pl.pallas_call(
        functools.partial(pack, order),
        out_shape=jax.ShapeDtypeStruct((FLIGHT, CAP, width), moe_in.dtype),
        in_specs=[pl.BlockSpec(memory_space=pltpu.HBM)] * 2,
        out_specs=VMEM,
        scratch_shapes=[
            pltpu.VMEM(routes_t.shape, routes_t.dtype),
            pltpu.VMEM(moe_in.shape, moe_in.dtype),
            pltpu.SemaphoreType.DMA((2,)),
        ],
        compiler_params=SMALL,
        cost_estimate=pl.CostEstimate(
            flops=AHEAD * (w_gate.nbytes + w_up.nbytes + w_down.nbytes),
            bytes_accessed=0,
            transcendentals=0,
        ),
        name="pack",
    )(far(routes_t), far(moe_in))
    if copies > 1:
        outgoing = jnp.broadcast_to(outgoing[:, None], (FLIGHT, copies, CAP, width)).reshape(
            n, CAP, width
        )
    arrived = exchange(outgoing)
    columns = w_gate.shape[1]
    parts = 2 if columns % (2 * LANES) == 0 else 1
    cores = lax.axis_size("head")
    swap = [(i, (i + 1) % cores) for i in range(cores)]
    near_gate, near_up, near_down = near(w_gate), near(w_up), near(w_down)
    own, other = [], []
    for part in range(parts):
        own.append(
            call(
                functools.partial(gate_up, part),
                jax.ShapeDtypeStruct((2, n * CAP, columns // parts), jnp.float32),
                arrived, near_gate, near_up,
                flops=4 * n * CAP * w_gate.size // parts,
            )
        )
        other.append(lax.ppermute(own[-1], "head", swap))
    totals = ()
    for part in range(parts - 1):
        totals = (
            call(
                functools.partial(down, part, ()),
                jax.ShapeDtypeStruct((n * CAP, width), jnp.float32),
                near_down, own[part], other[part], *totals,
                flops=2 * n * CAP * w_down.size // parts,
            ),
        )
    partial_out, terms = call(
        functools.partial(down, parts - 1, order),
        (
            jax.ShapeDtypeStruct((n, CAP, width), moe_in.dtype),
            jax.ShapeDtypeStruct((FLIGHT * CAP, 3 * rows), jnp.bfloat16),
        ),
        near_down, own[-1], other[-1], *totals, routes_t, gates_t,
        flops=2 * n * CAP * w_down.size // parts,
    )
    returned = exchange(partial_out)
    if copies > 1:
        returned = jnp.sum(
            returned.reshape(FLIGHT, copies, CAP, width).astype(jnp.float32), axis=1
        )
    return call(unpack, jax.ShapeDtypeStruct((rows, width), moe_in.dtype), terms, returned)


def solution(mesh):
    in_specs = (
        P(("groups", "expert"), "head"),
        P(("groups", "expert"), None),
        P(("groups", "expert"), None),
        P("head", "expert"),
        P("head", "expert"),
        P("expert", "head"),
    )
    out_specs = P(("groups", "expert"), "head")
    return jax.shard_map(
        per_device, mesh=mesh, in_specs=in_specs, out_specs=out_specs, check_vma=False
    )
```

```python
import functools

import jax
import jax.numpy as jnp
from jax import lax
from jax.experimental import pallas as pl
from jax.experimental.pallas import tpu as pltpu
from jax.sharding import PartitionSpec as P

FLIGHT = 8
CAP = 2
TILE = 512
LANES = 128
ORDERS = {8: (5, 0, 2, 7, 1, 3, 6, 4)}
AHEAD = 450
SMALL = pltpu.CompilerParams(vmem_limit_bytes=4 << 20)
VMEM = pl.BlockSpec(memory_space=pltpu.VMEM)


def near(array):
    return pltpu.with_memory_space_constraint(array, pltpu.VMEM)


def far(array):
    return pltpu.with_memory_space_constraint(array, pltpu.HBM)


def call(kernel, out_shape, *operands, flops=0):
    return pl.pallas_call(
        kernel,
        out_shape=out_shape,
        in_specs=[VMEM] * len(operands),
        out_specs=jax.tree.map(lambda _: VMEM, out_shape),
        compiler_params=SMALL,
        cost_estimate=pl.CostEstimate(flops=flops, bytes_accessed=0, transcendentals=0),
        name=getattr(kernel, "func", kernel).__name__,
    )(*operands)


def experts_of(order, shape):
    slot = lax.broadcasted_iota(jnp.int32, shape, 0)
    block = lax.div(slot, CAP)
    expert = jnp.zeros(shape, jnp.int32)
    for place, name in enumerate(order):
        expert = jnp.where(block == place, name, expert)
    return expert, slot - block * CAP


def placing(routes, order):
    rows = routes.shape[1]
    expert, number = experts_of(order, (len(order) * CAP, rows))
    chosen = (routes[0:1, :] == expert).astype(jnp.float32)
    for k in range(1, routes.shape[0]):
        chosen += (routes[k : k + 1, :] == expert).astype(jnp.float32)
    earlier = (
        lax.broadcasted_iota(jnp.int32, (rows, rows), 0)
        < lax.broadcasted_iota(jnp.int32, (rows, rows), 1)
    ).astype(jnp.float32)
    rank = jnp.dot(chosen, earlier, preferred_element_type=jnp.float32)
    return chosen * (rank == number.astype(jnp.float32)).astype(jnp.float32)


def pack(order, routes_hbm, rows_hbm, out_ref, routes_ref, rows_ref, sems):
    loads = [
        pltpu.make_async_copy(routes_hbm, routes_ref, sems.at[0]),
        pltpu.make_async_copy(rows_hbm, rows_ref, sems.at[1]),
    ]
    for load in loads:
        load.start()
    loads[0].wait()
    place = placing(routes_ref[...], order).astype(jnp.bfloat16)
    loads[1].wait()
    packed = jnp.dot(place, rows_ref[...], preferred_element_type=jnp.float32).astype(
        out_ref.dtype
    )
    out_ref[...] = packed.reshape(out_ref.shape)


def project(blocks, *refs):
    *weights, rows_ref, out_ref = refs
    columns = out_ref.shape[2]
    tile = min(TILE, columns)
    rows = rows_ref[...].reshape(-1, rows_ref.shape[-1])
    for block, (which, part) in enumerate(blocks):
        for start in range(0, columns, tile):
            out_ref[block, :, start : start + tile] = jnp.dot(
                rows,
                weights[which][:, part * columns + start : part * columns + start + tile],
                preferred_element_type=jnp.float32,
            )


def spread(routes, gates, order):
    place = placing(routes, order)
    expert, _ = experts_of(order, place.shape)
    weight = jnp.zeros(place.shape, jnp.float32)
    for k in range(routes.shape[0]):
        weight += jnp.where(routes[k : k + 1, :] == expert, gates[k : k + 1, :], 0.0)
    rest, terms = place * weight, []
    for _ in range(3):
        terms.append(rest.astype(jnp.bfloat16))
        rest = rest - terms[-1].astype(jnp.float32)
    return jnp.concatenate(terms, axis=1)


def down(part, order, gate_block, up_block, down_ref, *refs):
    gate_ref, gate_other, up_ref, up_other, *refs = refs
    columns = up_ref.shape[2]
    gate = gate_ref[gate_block] + gate_other[gate_block]
    up = up_ref[up_block] + up_other[up_block]
    hidden = (gate / (1.0 + jnp.exp(-gate)) * up).astype(jnp.bfloat16)
    width = down_ref.shape[1]
    tile = min(TILE, width)
    if order:
        *totals, routes_ref, gates_ref, out_ref, terms_ref = refs
        terms_ref[...] = spread(routes_ref[...], gates_ref[...], order)
    else:
        *totals, out_ref = refs
    for start in range(0, width, tile):
        at = slice(start, start + tile)
        total = jnp.dot(
            hidden,
            down_ref[part * columns : (part + 1) * columns, at],
            preferred_element_type=jnp.float32,
        )
        if totals:
            total += totals[0][:, at]
        out_ref[..., at] = total.astype(out_ref.dtype).reshape(*out_ref.shape[:-1], tile)


def unpack(terms_ref, slots_ref, out_ref):
    experts, cap, width = slots_ref.shape
    sums = lax.dot_general(
        terms_ref[...],
        slots_ref[...].astype(jnp.bfloat16).reshape(experts * cap, width),
        (((0,), (0,)), ((), ())),
        preferred_element_type=jnp.float32,
    )
    rows = out_ref.shape[0]
    out_ref[...] = (sums[:rows] + sums[rows : 2 * rows] + sums[2 * rows :]).astype(out_ref.dtype)


def per_device(moe_in, routes, gate_weights, w_gate, w_up, w_down):
    rows, width = moe_in.shape
    routes_t, gates_t = routes.T, gate_weights.T
    n = lax.axis_size("expert")
    copies = n // FLIGHT
    order = ORDERS.get(n, tuple(range(FLIGHT)))
    exchange = functools.partial(
        lax.all_to_all, axis_name="expert", split_axis=0, concat_axis=0, tiled=True,
        axis_index_groups=[list(order)] if copies == 1 else None,
    )
    outgoing = pl.pallas_call(
        functools.partial(pack, order),
        out_shape=jax.ShapeDtypeStruct((FLIGHT, CAP, width), moe_in.dtype),
        in_specs=[pl.BlockSpec(memory_space=pltpu.HBM)] * 2,
        out_specs=VMEM,
        scratch_shapes=[
            pltpu.VMEM(routes_t.shape, routes_t.dtype),
            pltpu.VMEM(moe_in.shape, moe_in.dtype),
            pltpu.SemaphoreType.DMA((2,)),
        ],
        compiler_params=SMALL,
        cost_estimate=pl.CostEstimate(
            flops=AHEAD * (w_gate.nbytes + w_up.nbytes + w_down.nbytes),
            bytes_accessed=0,
            transcendentals=0,
        ),
        name="pack",
    )(far(routes_t), far(moe_in))
    if copies > 1:
        outgoing = jnp.broadcast_to(outgoing[:, None], (FLIGHT, copies, CAP, width)).reshape(
            n, CAP, width
        )
    arrived = exchange(outgoing)
    columns = w_gate.shape[1]
    parts = 2 if columns % (2 * LANES) == 0 else 1
    cores = lax.axis_size("head")
    swap = [(i, (i + 1) % cores) for i in range(cores)]
    near_gate, near_up, near_down = near(w_gate), near(w_up), near(w_down)

    def swapped(blocks, *weights):
        product = call(
            functools.partial(project, blocks),
            jax.ShapeDtypeStruct((len(blocks), n * CAP, columns // parts), jnp.float32),
            *weights, arrived,
            flops=2 * n * CAP * len(blocks) * w_gate.size // parts,
        )
        return product, lax.ppermute(product, "head", swap)

    first = swapped([(1, part) for part in range(parts)] + [(0, 0)], near_up, near_gate)
    later = [swapped([(0, part)], near_up) for part in range(1, parts)]
    places = [(first, parts)] + [(pair, 0) for pair in later]
    totals = ()
    for part in range(parts - 1):
        totals = (
            call(
                functools.partial(down, part, (), part, places[part][1]),
                jax.ShapeDtypeStruct((n * CAP, width), jnp.float32),
                near_down, *first, *places[part][0], *totals,
                flops=2 * n * CAP * w_down.size // parts,
            ),
        )
    partial_out, terms = call(
        functools.partial(down, parts - 1, order, parts - 1, places[-1][1]),
        (
            jax.ShapeDtypeStruct((n, CAP, width), moe_in.dtype),
            jax.ShapeDtypeStruct((FLIGHT * CAP, 3 * rows), jnp.bfloat16),
        ),
        near_down, *first, *places[-1][0], *totals, routes_t, gates_t,
        flops=2 * n * CAP * w_down.size // parts,
    )
    returned = exchange(partial_out)
    if copies > 1:
        returned = jnp.sum(
            returned.reshape(FLIGHT, copies, CAP, width).astype(jnp.float32), axis=1
        )
    return call(unpack, jax.ShapeDtypeStruct((rows, width), moe_in.dtype), terms, returned)


def solution(mesh):
    in_specs = (
        P(("groups", "expert"), "head"),
        P(("groups", "expert"), None),
        P(("groups", "expert"), None),
        P("head", "expert"),
        P("head", "expert"),
        P("expert", "head"),
    )
    out_specs = P(("groups", "expert"), "head")
    return jax.shard_map(
        per_device, mesh=mesh, in_specs=in_specs, out_specs=out_specs, check_vma=False
    )
```

```python
import functools

import jax
import jax.numpy as jnp
from jax import lax
from jax.experimental import pallas as pl
from jax.experimental.pallas import tpu as pltpu
from jax.sharding import PartitionSpec as P

FLIGHT = 8
CAP = 2
TILE = 512
LANES = 128
ORDERS = {8: (5, 0, 2, 7, 1, 3, 6, 4)}
AHEAD = 450
SMALL = pltpu.CompilerParams(vmem_limit_bytes=4 << 20)
VMEM = pl.BlockSpec(memory_space=pltpu.VMEM)


def near(array):
    return pltpu.with_memory_space_constraint(array, pltpu.VMEM)


def far(array):
    return pltpu.with_memory_space_constraint(array, pltpu.HBM)


def call(kernel, out_shape, *operands, flops=0):
    return pl.pallas_call(
        kernel,
        out_shape=out_shape,
        in_specs=[VMEM] * len(operands),
        out_specs=jax.tree.map(lambda _: VMEM, out_shape),
        compiler_params=SMALL,
        cost_estimate=pl.CostEstimate(flops=flops, bytes_accessed=0, transcendentals=0),
        name=getattr(kernel, "func", kernel).__name__,
    )(*operands)


def experts_of(order, shape):
    slot = lax.broadcasted_iota(jnp.int32, shape, 0)
    block = lax.div(slot, CAP)
    expert = jnp.zeros(shape, jnp.int32)
    for place, name in enumerate(order):
        expert = jnp.where(block == place, name, expert)
    return expert, slot - block * CAP


def placing(routes, order):
    rows = routes.shape[1]
    expert, number = experts_of(order, (len(order) * CAP, rows))
    chosen = (routes[0:1, :] == expert).astype(jnp.float32)
    for k in range(1, routes.shape[0]):
        chosen += (routes[k : k + 1, :] == expert).astype(jnp.float32)
    earlier = (
        lax.broadcasted_iota(jnp.int32, (rows, rows), 0)
        < lax.broadcasted_iota(jnp.int32, (rows, rows), 1)
    ).astype(jnp.float32)
    rank = jnp.dot(chosen, earlier, preferred_element_type=jnp.float32)
    return chosen * (rank == number.astype(jnp.float32)).astype(jnp.float32)


def pack(order, routes_hbm, rows_hbm, out_ref, routes_ref, rows_ref, sems):
    loads = [
        pltpu.make_async_copy(routes_hbm, routes_ref, sems.at[0]),
        pltpu.make_async_copy(rows_hbm, rows_ref, sems.at[1]),
    ]
    for load in loads:
        load.start()
    loads[0].wait()
    place = placing(routes_ref[...], order).astype(jnp.bfloat16)
    loads[1].wait()
    packed = jnp.dot(place, rows_ref[...], preferred_element_type=jnp.float32).astype(
        out_ref.dtype
    )
    out_ref[...] = packed.reshape(out_ref.shape)


def project(blocks, *refs):
    *weights, rows_ref, out_ref = refs
    columns = out_ref.shape[2]
    tile = min(TILE, columns)
    rows = rows_ref[...].reshape(-1, rows_ref.shape[-1])
    for block, (which, part) in enumerate(blocks):
        for start in range(0, columns, tile):
            out_ref[block, :, start : start + tile] = jnp.dot(
                rows,
                weights[which][:, part * columns + start : part * columns + start + tile],
                preferred_element_type=jnp.float32,
            )


def spread(routes, gates, order):
    place = placing(routes, order)
    expert, _ = experts_of(order, place.shape)
    weight = jnp.zeros(place.shape, jnp.float32)
    for k in range(routes.shape[0]):
        weight += jnp.where(routes[k : k + 1, :] == expert, gates[k : k + 1, :], 0.0)
    rest, terms = (place * weight).T, []
    for _ in range(3):
        terms.append(rest.astype(jnp.bfloat16))
        rest = rest - terms[-1].astype(jnp.float32)
    return jnp.concatenate(terms, axis=0)


def down(part, order, gate_block, up_block, down_ref, *refs):
    gate_ref, gate_other, up_ref, up_other, *refs = refs
    columns = up_ref.shape[2]
    gate = gate_ref[gate_block] + gate_other[gate_block]
    up = up_ref[up_block] + up_other[up_block]
    hidden = (gate / (1.0 + jnp.exp(-gate)) * up).astype(jnp.bfloat16)
    width = down_ref.shape[1]
    tile = min(TILE, width)
    if order:
        *totals, routes_ref, gates_ref, out_ref, terms_ref = refs
        terms_ref[...] = spread(routes_ref[...], gates_ref[...], order)
    else:
        *totals, out_ref = refs
    for start in range(0, width, tile):
        at = slice(start, start + tile)
        total = jnp.dot(
            hidden,
            down_ref[part * columns : (part + 1) * columns, at],
            preferred_element_type=jnp.float32,
        )
        if totals:
            total += totals[0][:, at]
        out_ref[..., at] = total.astype(out_ref.dtype).reshape(*out_ref.shape[:-1], tile)


def unpack(terms_ref, slots_ref, out_ref):
    experts, cap, width = slots_ref.shape
    rows = out_ref.shape[0]
    slots = slots_ref[...].reshape(experts * cap, width)
    if slots.dtype == jnp.bfloat16:
        sums = jnp.dot(terms_ref[...], slots, preferred_element_type=jnp.float32)
        total = sums[:rows] + sums[rows : 2 * rows] + sums[2 * rows :]
    else:
        terms = terms_ref[...].astype(jnp.float32)
        total = jnp.dot(
            terms[:rows] + terms[rows : 2 * rows] + terms[2 * rows :],
            slots,
            precision=lax.Precision.HIGHEST,
            preferred_element_type=jnp.float32,
        )
    out_ref[...] = total.astype(out_ref.dtype)


def per_device(moe_in, routes, gate_weights, w_gate, w_up, w_down):
    rows, width = moe_in.shape
    routes_t, gates_t = routes.T, gate_weights.T
    n = lax.axis_size("expert")
    copies = n // FLIGHT
    order = ORDERS.get(n, tuple(range(FLIGHT)))
    exchange = functools.partial(
        lax.all_to_all, axis_name="expert", split_axis=0, concat_axis=0, tiled=True,
        axis_index_groups=[list(order)] if copies == 1 else None,
    )
    outgoing = pl.pallas_call(
        functools.partial(pack, order),
        out_shape=jax.ShapeDtypeStruct((FLIGHT, CAP, width), moe_in.dtype),
        in_specs=[pl.BlockSpec(memory_space=pltpu.HBM)] * 2,
        out_specs=VMEM,
        scratch_shapes=[
            pltpu.VMEM(routes_t.shape, routes_t.dtype),
            pltpu.VMEM(moe_in.shape, moe_in.dtype),
            pltpu.SemaphoreType.DMA((2,)),
        ],
        compiler_params=SMALL,
        cost_estimate=pl.CostEstimate(
            flops=AHEAD * (w_gate.nbytes + w_up.nbytes + w_down.nbytes),
            bytes_accessed=0,
            transcendentals=0,
        ),
        name="pack",
    )(far(routes_t), far(moe_in))
    if copies > 1:
        outgoing = jnp.broadcast_to(outgoing[:, None], (FLIGHT, copies, CAP, width)).reshape(
            n, CAP, width
        )
    arrived = exchange(outgoing)
    columns = w_gate.shape[1]
    parts = 2 if columns % (2 * LANES) == 0 else 1
    cores = lax.axis_size("head")
    swap = [(i, (i + 1) % cores) for i in range(cores)]
    near_gate, near_up, near_down = near(w_gate), near(w_up), near(w_down)

    def swapped(blocks, *weights):
        product = call(
            functools.partial(project, blocks),
            jax.ShapeDtypeStruct((len(blocks), n * CAP, columns // parts), jnp.float32),
            *weights, arrived,
            flops=2 * n * CAP * len(blocks) * w_gate.size // parts,
        )
        return product, lax.ppermute(product, "head", swap)

    first = swapped([(1, part) for part in range(parts)] + [(0, 0)], near_up, near_gate)
    later = [swapped([(0, part)], near_up) for part in range(1, parts)]
    places = [(first, parts)] + [(pair, 0) for pair in later]
    totals = ()
    for part in range(parts - 1):
        totals = (
            call(
                functools.partial(down, part, (), part, places[part][1]),
                jax.ShapeDtypeStruct((n * CAP, width), jnp.float32),
                near_down, *first, *places[part][0], *totals,
                flops=2 * n * CAP * w_down.size // parts,
            ),
        )
    partial_out, terms = call(
        functools.partial(down, parts - 1, order, parts - 1, places[-1][1]),
        (
            jax.ShapeDtypeStruct((n, CAP, width), moe_in.dtype),
            jax.ShapeDtypeStruct((3 * rows, FLIGHT * CAP), jnp.bfloat16),
        ),
        near_down, *first, *places[-1][0], *totals, routes_t, gates_t,
        flops=2 * n * CAP * w_down.size // parts,
    )
    returned = exchange(partial_out)
    if copies > 1:
        returned = jnp.sum(
            returned.reshape(FLIGHT, copies, CAP, width).astype(jnp.float32), axis=1
        )
    return call(unpack, jax.ShapeDtypeStruct((rows, width), moe_in.dtype), terms, returned)


def solution(mesh):
    in_specs = (
        P(("groups", "expert"), "head"),
        P(("groups", "expert"), None),
        P(("groups", "expert"), None),
        P("head", "expert"),
        P("head", "expert"),
        P("expert", "head"),
    )
    out_specs = P(("groups", "expert"), "head")
    return jax.shard_map(
        per_device, mesh=mesh, in_specs=in_specs, out_specs=out_specs, check_vma=False
    )
```

```python
import functools

import jax
import jax.numpy as jnp
from jax import lax
from jax.experimental import pallas as pl
from jax.experimental.pallas import tpu as pltpu
from jax.sharding import PartitionSpec as P

FLIGHT = 8
CAP = 2
TILE = 512
LANES = 128
ORDERS = {8: (5, 0, 2, 7, 1, 3, 6, 4)}
AHEAD = 450
SMALL = pltpu.CompilerParams(vmem_limit_bytes=4 << 20)
VMEM = pl.BlockSpec(memory_space=pltpu.VMEM)


def near(array):
    return pltpu.with_memory_space_constraint(array, pltpu.VMEM)


def far(array):
    return pltpu.with_memory_space_constraint(array, pltpu.HBM)


def call(kernel, out_shape, *operands, flops=0):
    return pl.pallas_call(
        kernel,
        out_shape=out_shape,
        in_specs=[VMEM] * len(operands),
        out_specs=jax.tree.map(lambda _: VMEM, out_shape),
        compiler_params=SMALL,
        cost_estimate=pl.CostEstimate(flops=flops, bytes_accessed=0, transcendentals=0),
        name=getattr(kernel, "func", kernel).__name__,
    )(*operands)


def experts_of(order, shape):
    slot = lax.broadcasted_iota(jnp.int32, shape, 0)
    block = lax.div(slot, CAP)
    expert = jnp.zeros(shape, jnp.int32)
    for place, name in enumerate(order):
        expert = jnp.where(block == place, name, expert)
    return expert, slot - block * CAP


def placing(routes, order):
    rows = routes.shape[1]
    expert, number = experts_of(order, (len(order) * CAP, rows))
    chosen = (routes[0:1, :] == expert).astype(jnp.float32)
    for k in range(1, routes.shape[0]):
        chosen += (routes[k : k + 1, :] == expert).astype(jnp.float32)
    earlier = (
        lax.broadcasted_iota(jnp.int32, (rows, rows), 0)
        < lax.broadcasted_iota(jnp.int32, (rows, rows), 1)
    ).astype(jnp.float32)
    rank = jnp.dot(chosen, earlier, preferred_element_type=jnp.float32)
    return chosen * (rank == number.astype(jnp.float32)).astype(jnp.float32)


def pack(order, routes_hbm, rows_hbm, out_ref, routes_ref, rows_ref, sems):
    loads = [
        pltpu.make_async_copy(routes_hbm, routes_ref, sems.at[0]),
        pltpu.make_async_copy(rows_hbm, rows_ref, sems.at[1]),
    ]
    for load in loads:
        load.start()
    loads[0].wait()
    place = placing(routes_ref[...], order).astype(jnp.bfloat16)
    loads[1].wait()
    packed = jnp.dot(place, rows_ref[...], preferred_element_type=jnp.float32).astype(
        out_ref.dtype
    )
    out_ref[...] = packed.reshape(out_ref.shape)


def project(blocks, *refs):
    *weights, rows_ref, out_ref = refs
    columns = out_ref.shape[2]
    tile = min(TILE, columns)
    rows = rows_ref[...].reshape(-1, rows_ref.shape[-1])
    for block, (which, part) in enumerate(blocks):
        for start in range(0, columns, tile):
            out_ref[block, :, start : start + tile] = jnp.dot(
                rows,
                weights[which][:, part * columns + start : part * columns + start + tile],
                preferred_element_type=jnp.float32,
            )


def spread(routes, gates, order):
    place = placing(routes, order)
    expert, _ = experts_of(order, place.shape)
    weight = jnp.zeros(place.shape, jnp.float32)
    for k in range(routes.shape[0]):
        weight += jnp.where(routes[k : k + 1, :] == expert, gates[k : k + 1, :], 0.0)
    rest, terms = (place * weight).T, []
    for _ in range(3):
        terms.append(rest.astype(jnp.bfloat16))
        rest = rest - terms[-1].astype(jnp.float32)
    return jnp.concatenate(terms, axis=0)


def down(part, order, gate_block, up_block, gate_ref, down_ref, *refs):
    gate_other, up_ref, up_other, *refs = refs
    columns = up_ref.shape[2]
    gate = gate_ref[gate_block] + gate_other[gate_block]
    up = up_ref[up_block] + up_other[up_block]
    hidden = (gate / (1.0 + jnp.exp(-gate)) * up).astype(jnp.bfloat16)
    width = down_ref.shape[1]
    tile = min(TILE, width)
    if order:
        *totals, routes_ref, gates_ref, out_ref, terms_ref = refs
        terms_ref[...] = spread(routes_ref[...], gates_ref[...], order)
    else:
        *totals, out_ref = refs
    for start in range(0, width, tile):
        at = slice(start, start + tile)
        total = jnp.dot(
            hidden,
            down_ref[part * columns : (part + 1) * columns, at],
            preferred_element_type=jnp.float32,
        )
        if totals:
            total += totals[0][:, at]
        out_ref[..., at] = total.astype(out_ref.dtype).reshape(*out_ref.shape[:-1], tile)


def unpack(terms_ref, slots_ref, out_ref):
    experts, cap, width = slots_ref.shape
    rows = out_ref.shape[0]
    slots = slots_ref[...].reshape(experts * cap, width)
    if slots.dtype == jnp.bfloat16:
        sums = jnp.dot(terms_ref[...], slots, preferred_element_type=jnp.float32)
        total = sums[:rows] + sums[rows : 2 * rows] + sums[2 * rows :]
    else:
        terms = terms_ref[...].astype(jnp.float32)
        total = jnp.dot(
            terms[:rows] + terms[rows : 2 * rows] + terms[2 * rows :],
            slots,
            precision=lax.Precision.HIGHEST,
            preferred_element_type=jnp.float32,
        )
    out_ref[...] = total.astype(out_ref.dtype)


def per_device(moe_in, routes, gate_weights, w_gate, w_up, w_down):
    rows, width = moe_in.shape
    routes_t, gates_t = routes.T, gate_weights.T
    n = lax.axis_size("expert")
    copies = n // FLIGHT
    order = ORDERS.get(n, tuple(range(FLIGHT)))
    exchange = functools.partial(
        lax.all_to_all, axis_name="expert", split_axis=0, concat_axis=0, tiled=True,
        axis_index_groups=[list(order)] if copies == 1 else None,
    )
    outgoing = pl.pallas_call(
        functools.partial(pack, order),
        out_shape=jax.ShapeDtypeStruct((FLIGHT, CAP, width), moe_in.dtype),
        in_specs=[pl.BlockSpec(memory_space=pltpu.HBM)] * 2,
        out_specs=VMEM,
        scratch_shapes=[
            pltpu.VMEM(routes_t.shape, routes_t.dtype),
            pltpu.VMEM(moe_in.shape, moe_in.dtype),
            pltpu.SemaphoreType.DMA((2,)),
        ],
        compiler_params=SMALL,
        cost_estimate=pl.CostEstimate(
            flops=AHEAD * (w_gate.nbytes + w_up.nbytes + w_down.nbytes),
            bytes_accessed=0,
            transcendentals=0,
        ),
        name="pack",
    )(far(routes_t), far(moe_in))
    if copies > 1:
        outgoing = jnp.broadcast_to(outgoing[:, None], (FLIGHT, copies, CAP, width)).reshape(
            n, CAP, width
        )
    arrived = exchange(outgoing)
    columns = w_gate.shape[1]
    parts = 2 if columns % (2 * LANES) == 0 else 1
    cores = lax.axis_size("head")
    swap = [(i, (i + 1) % cores) for i in range(cores)]
    near_gate, near_up, near_down = near(w_gate), near(w_up), near(w_down)

    def swapped(blocks, *weights):
        product = call(
            functools.partial(project, blocks),
            jax.ShapeDtypeStruct((len(blocks), n * CAP, columns // parts), jnp.float32),
            *weights, arrived,
            flops=2 * n * CAP * len(blocks) * w_gate.size // parts,
        )
        return product, lax.ppermute(product, "head", swap)

    first = swapped([(1, part) for part in range(parts)] + [(0, 0)], near_up, near_gate)
    later = [swapped([(0, part)], near_up, near_down) for part in range(1, parts)]
    places = [(first, parts)] + [(pair, 0) for pair in later]
    totals = ()
    for part in range(parts - 1):
        totals = (
            call(
                functools.partial(down, part, (), part, places[part][1]),
                jax.ShapeDtypeStruct((n * CAP, width), jnp.float32),
                first[0], near_down, first[1], *places[part][0], *totals,
                flops=2 * n * CAP * w_down.size // parts,
            ),
        )
    partial_out, terms = call(
        functools.partial(down, parts - 1, order, parts - 1, places[-1][1]),
        (
            jax.ShapeDtypeStruct((n, CAP, width), moe_in.dtype),
            jax.ShapeDtypeStruct((3 * rows, FLIGHT * CAP), jnp.bfloat16),
        ),
        first[0], near_down, first[1], *places[-1][0], *totals, routes_t, gates_t,
        flops=2 * n * CAP * w_down.size // parts,
    )
    returned = exchange(partial_out)
    if copies > 1:
        returned = jnp.sum(
            returned.reshape(FLIGHT, copies, CAP, width).astype(jnp.float32), axis=1
        )
    return call(unpack, jax.ShapeDtypeStruct((rows, width), moe_in.dtype), terms, returned)


def solution(mesh):
    in_specs = (
        P(("groups", "expert"), "head"),
        P(("groups", "expert"), None),
        P(("groups", "expert"), None),
        P("head", "expert"),
        P("head", "expert"),
        P("expert", "head"),
    )
    out_specs = P(("groups", "expert"), "head")
    return jax.shard_map(
        per_device, mesh=mesh, in_specs=in_specs, out_specs=out_specs, check_vma=False
    )
```
